256 devices in a mesh: row: 32 (over x, z), col: 8 (over y, core).
Axes of the slice: x: 4, y: 4, z: 8, core: 2. Of those that a mesh axis runs over, the one named last changes fastest.
Arguments:
- tile_vals: bfloat16 [32, 8, 256, 128, 128], P('row', 'col'), may hold values from -0.25 to 0.25
- tile_row: int32 [32, 8, 256], P('row', 'col'), may hold values from 0 to 31
- tile_col: int32 [32, 8, 256], P('row', 'col'), may hold values from 0 to 127
- tile_count: int32 [32, 8], P('row', 'col'), may hold values from 64 to 256
- out_grad: bfloat16 [131072, 128], P('row', 'col'), may hold values from -6 to 6
- relu_mask: int32 [131072, 128], P('row', 'col'), may hold values 0 or 1
- features: bfloat16 [131072, 128], P(('row', 'col')), may hold values from -6 to 6
- weight: bfloat16 [128, 128], replicated, may hold values from -0.5 to 0.5
- importance: float32 [128, 128], replicated, may hold values from 0 to 1
- weight_delta: float32 [128, 128], replicated, may hold values from -0.016572814 to 0.016572814
Outputs:
- input_grad: bfloat16 [131072, 128], P(('row', 'col'))
- importance_out: float32 [128, 128], replicated
The draws below stay inside these ranges and needn't reach their ends.
All inputs are finite; a program needn't handle non-finite values. No bound on the sum of `relu_mask` on one device may be relied on, other than what follows from the above.
Results may differ from the reference program's by a relative error of at most 0.022.
Values may be sent and summed in bfloat16 or wider, within the bound.
No kernel may reach another device: no remote copies, remote signals or barrier semaphores. Data moves between devices by JAX's collectives and lax.ppermute only.
A program may use at most 128 MiB of HBM per device.

```python
import jax
import jax.numpy as jnp
from jax import lax

F = 128
D_IN = 128
TILE = 128
NB = 512
TILES = 256
NODES = 131072
ROWT = 32
COLT = 128
N_ROW = 32
N_COL = 8


def draw_tile_count(key, part):
    key = jax.random.fold_in(key, 7)
    first_key, second_key = jax.random.split(key)
    counts = jax.random.randint(first_key, (N_ROW, N_COL), TILES // 4, TILES + 1)
    chosen = jax.random.randint(second_key, (), 0, N_ROW * N_COL)
    flat_counts = counts.reshape(-1).at[chosen].set(TILES)
    return flat_counts.reshape(N_ROW, N_COL).astype(jnp.int32)


def with_ends(drawn, stream_key, smallest, largest):
    place = [jax.random.randint(jax.random.fold_in(stream_key, axis), (), 0, length) for axis, length in enumerate(drawn.shape)]
    longest = drawn.shape.index(max(drawn.shape))
    beside = place[:longest] + [(place[longest] + 1) % drawn.shape[longest]] + place[longest + 1:]
    return drawn.at[tuple(place)].set(smallest).at[tuple(beside)].set(largest)


def levels(stream_key, dims, shards, low, top_value):
    loudness, own = 1.0, jax.random.fold_in(stream_key, 6)
    for position, shards_of in shards:
        steps = jnp.exp(jax.random.uniform(jax.random.fold_in(own, position), (shards_of,), jnp.float32, low / len(shards), top_value / len(shards)))
        loudness = loudness * jnp.repeat(steps, dims[position] // shards_of).reshape([-1 if axis == position else 1 for axis in range(len(dims))])
    return loudness


def gaussian(key, dims, deviation, most, pieces=(), kind=jnp.bfloat16):
    result = deviation * jax.random.normal(key, dims, jnp.float32)
    if pieces:
        result = result * levels(key, dims, pieces, -0.22, 0.18)
    return jnp.clip(result, -most, most).astype(kind)


def setup_inputs(seed: int = 0) -> dict:
    key_of = jax.random.split(jax.random.key(seed), 11)
    return {
        "tile_vals": gaussian(key_of[0], (N_ROW, N_COL, TILES, TILE, TILE), (TILE * TILES * 2 // COLT) ** -0.5, 0.25, ((0, 32), (1, 8))),
        "tile_row": with_ends(jax.random.randint(key_of[1], (N_ROW, N_COL, TILES), 0, ROWT), jax.random.fold_in(key_of[1], 1), 0, ROWT - 1).astype(jnp.int32),
        "tile_col": with_ends(jax.random.randint(key_of[2], (N_ROW, N_COL, TILES), 0, COLT), jax.random.fold_in(key_of[2], 1), 0, COLT - 1).astype(jnp.int32),
        "tile_count": draw_tile_count(jax.random.fold_in(key_of[10], 71), 0),
        "out_grad": gaussian(key_of[4], (NODES, F), 1.0, 6.0, ((0, 32), (1, 8))),
        "relu_mask": with_ends((jax.random.randint(key_of[5], (NODES, F), 0, 2) < 1).astype(jnp.int32), jax.random.fold_in(key_of[5], 1), 0, 1),
        "features": gaussian(key_of[6], (NODES, D_IN), 1.0, 6.0, ((0, 256),)),
        "weight": gaussian(key_of[7], (D_IN, F), F ** -0.5, 0.5),
        "importance": jnp.clip(jax.random.uniform(key_of[8], (D_IN, F), jnp.float32, 0.0, 1.0), 0.0, 1.0),
        "weight_delta": gaussian(key_of[9], (D_IN, F), (NODES ** -0.5), 0.016572814, (), jnp.float32),
    }


def reference(tile_vals, tile_row, tile_col, tile_count, out_grad, relu_mask, features, weight, importance, weight_delta):
    masked = (out_grad.astype(jnp.float32) * relu_mask.astype(jnp.float32)).astype(jnp.bfloat16)
    row_blocks = masked.reshape(N_ROW, ROWT, TILE, F)
    flat_vals = tile_vals.reshape(N_ROW * N_COL, TILES, TILE, TILE)
    flat_rows = tile_row.reshape(N_ROW * N_COL, TILES)
    flat_cols = tile_col.reshape(N_ROW * N_COL, TILES)
    flat_count = tile_count.reshape(N_ROW * N_COL)
    per_block = NB // TILE
    column_index = jnp.arange(COLT, dtype=jnp.int32)

    def device_step(aggregate, device):
        row_pos = device // N_COL
        col_pos = device % N_COL
        picked = row_blocks[row_pos][flat_rows[device]]
        product = jnp.einsum("tij,tif->tjf", flat_vals[device].astype(jnp.float32), picked.astype(jnp.float32))
        usable = (jnp.arange(TILES, dtype=jnp.int32) < flat_count[device]).astype(jnp.float32)
        product = product * usable[:, None, None]
        partial_value = jnp.zeros((COLT, TILE, F), jnp.float32).at[flat_cols[device]].add(product)
        partial_b = lax.optimization_barrier(partial_value.astype(jnp.bfloat16)).astype(jnp.float32)
        target = ((column_index * TILE) // NB * N_COL + col_pos) * per_block + ((column_index * TILE) % NB) // TILE
        aggregate = aggregate.at[target.astype(jnp.int32)].add(partial_b)
        return aggregate, None

    start_agg = jnp.zeros((NODES // TILE, TILE, F), jnp.float32)
    aggregate, _ = lax.scan(device_step, start_agg, jnp.arange(N_ROW * N_COL, dtype=jnp.int32))
    aggregate_b = aggregate.reshape(NODES, F).astype(jnp.bfloat16)
    input_grad = jnp.dot(aggregate_b, weight.T, preferred_element_type=jnp.float32).astype(jnp.bfloat16)
    weight_grad = jnp.dot(features.T, aggregate_b, preferred_element_type=jnp.float32)
    importance_out = importance - weight_grad * weight_delta
    return input_grad, importance_out
```

```python
import functools

import jax
import jax.numpy as jnp
from jax import lax
from jax.experimental import pallas as pl
from jax.experimental.pallas import tpu as pltpu
from jax.sharding import Mesh, PartitionSpec as P

XS, ZS, YS, CS = 4, 8, 4, 2
T = 128
GROUP = 32
UNROLL = 8
F32, BF16 = jnp.float32, jnp.bfloat16


def shift(value, axis, size, by):
    return lax.ppermute(value, axis, [(i, (i + by) % size) for i in range(size)])


def tile_kernel(rows, places, meta, tiles, mine, other, c0, c1, c2a, c2b, c3, wide, acc):
    step = pl.program_id(0)

    @pl.when(step == 0)
    def _():
        for part, dist in enumerate((0, 1, 3, 2)):
            y_of = (meta[1] - dist) & (YS - 1)
            for ref, core in ((mine, meta[2]), (other, 1 - meta[2])):
                at = pl.multiple_of((y_of * CS + core) * 16, 16)
                wide[pl.ds(at, 16), :] = ref[part * 16 : part * 16 + 16, :]

        def clear(i, _):
            acc[pl.ds(i * 4, 4)] = jnp.zeros((4, T, T), F32)
            return 0

        lax.fori_loop(0, 32, clear, 0)

    def several(g, _):
        base = step * GROUP + g * UNROLL
        products = []
        for u in range(UNROLL):
            at = pl.multiple_of(rows[base + u] * T, T)
            products.append(
                jnp.dot(wide[:, pl.ds(at, T)], tiles[g * UNROLL + u], preferred_element_type=F32)
            )
        for u in range(UNROLL):
            place = places[base + u]
            acc[place] = acc[place] + products[u]
        return 0

    used = jnp.clip(meta[0] - step * GROUP, 0, GROUP)
    lax.fori_loop(0, (used + UNROLL - 1) >> 3, several, 0)

    @pl.when(step == pl.num_programs(0) - 1)
    def _():
        for out, first, size in ((c2a, 64, 16), (c2b, 80, 16), (c1, 32, 32), (c3, 96, 32), (c0, 0, 32)):

            def put(i, _):
                out[pl.ds(i * 4, 4)] = acc[pl.ds(first + i * 4, 4)].astype(BF16)
                return 0

            lax.fori_loop(0, size // 4, put, 0)


def tile_products(rows, places, meta, tiles, mine, other):
    steps = tiles.shape[0] // GROUP
    sizes = (32, 32, 16, 16, 32)
    whole = lambda shape: pl.BlockSpec(shape, lambda i, *_: (0,) * len(shape))
    return pl.pallas_call(
        tile_kernel,
        grid_spec=pltpu.PrefetchScalarGridSpec(
            num_scalar_prefetch=3,
            grid=(steps,),
            in_specs=[
                pl.BlockSpec((GROUP, T, T), lambda i, *_: (i, 0, 0)),
                whole(mine.shape),
                whole(other.shape),
            ],
            out_specs=[whole((n, T, T)) for n in sizes],
            scratch_shapes=[pltpu.VMEM((T, mine.shape[1]), BF16), pltpu.VMEM((129, T, T), F32)],
        ),
        out_shape=[jax.ShapeDtypeStruct((n, T, T), BF16) for n in sizes],
        compiler_params=pltpu.CompilerParams(vmem_limit_bytes=40 * 2**20),
        cost_estimate=pl.CostEstimate(flops=2**30, bytes_accessed=13 * 2**20, transcendentals=0),
    )(rows, places, meta, tiles, mine, other)


def middle_kernel(meta, c0, up, down, feats, z4a, z4b, z3, z5, z2, z6, z1, z7, z0, grad):
    total = jnp.zeros((T, T), F32)
    outs = {0: z0, 1: z1, 2: z2, 3: z3, 5: z5, 6: z6, 7: z7}
    for dist in range(ZS):
        z_of = (meta[3] + dist) & (ZS - 1)
        for q in range(4):
            n = dist * 4 + q
            value = (c0[n].astype(F32) + up[n].astype(F32) + down[n].astype(F32)).astype(BF16)
            if dist == 4:
                (z4a if q < 2 else z4b)[q % 2] = value
            else:
                outs[dist][q] = value
            total += jnp.dot(value, feats[z_of * 4 + q], preferred_element_type=F32)
    grad[...] = total


def middle(meta, c0, up, down, feats):
    sizes = (2, 2, 4, 4, 4, 4, 4, 4, 4)
    spec = pl.BlockSpec(memory_space=pltpu.VMEM)
    return pl.pallas_call(
        middle_kernel,
        in_specs=[pl.BlockSpec(memory_space=pltpu.SMEM)] + [spec] * 4,
        out_specs=[spec] * 10,
        out_shape=[jax.ShapeDtypeStruct((n, T, T), BF16) for n in sizes]
        + [jax.ShapeDtypeStruct((T, T), F32)],
        compiler_params=pltpu.CompilerParams(vmem_limit_bytes=24 * 2**20),
        cost_estimate=pl.CostEstimate(flops=2**27, bytes_accessed=5 * 2**20, transcendentals=0),
    )(meta, c0, up, down, feats)


def add(*values):
    return sum(v.astype(F32) for v in values).astype(BF16)


def local(tile_vals, tile_row, tile_col, tile_count, out_grad, relu_mask, features, weight, importance, weight_delta):
    x, z, y, core = (lax.axis_index(a) for a in ("x", "z", "y", "core"))
    slots = tile_vals.shape[2]
    wide_feats = lax.all_gather(features, "z", axis=0, tiled=True).reshape(ZS * 4, T, T)

    masked = (out_grad.astype(F32) * relu_mask.astype(F32)).astype(BF16).T
    mine = jnp.concatenate([masked] + [shift(masked, "y", YS, d) for d in (1, 3, 2)], axis=0)
    other = lax.ppermute(mine, "core", [(0, 1), (1, 0)])

    count = tile_count.reshape(())
    cols = tile_col.reshape(slots)
    dest = cols >> 2
    dx = ((dest >> 3) - x) & (XS - 1)
    dz = ((dest & 7) - z) & (ZS - 1)
    places = jnp.where(lax.iota(jnp.int32, slots) < count, (dx * ZS + dz) * 4 + (cols & 3), 128)
    meta = jnp.stack([count, y, core, z]).astype(jnp.int32)
    c0, c1, c2a, c2b, c3 = tile_products(
        tile_row.reshape(slots), places, meta, tile_vals.reshape(slots, T, T), mine, other
    )

    up, down = shift(c2a, "x", XS, 1), shift(c2b, "x", XS, 3)
    s1 = jnp.concatenate([add(c1[:16], up), c1[16:]], axis=0)
    s3 = jnp.concatenate([c3[:16], add(c3[16:], down)], axis=0)
    z4a, z4b, z3, z5, z2, z6, z1, z7, z0, grad = middle(
        meta, c0, shift(s1, "x", XS, 1), shift(s3, "x", XS, 3), wide_feats
    )

    up, down = shift(z4a, "z", ZS, 1), shift(z4b, "z", ZS, 7)
    up = jnp.concatenate([add(z3[:2], up), z3[2:]], axis=0)
    down = jnp.concatenate([z5[:2], add(z5[2:], down)], axis=0)
    for u, d in ((z2, z6), (z1, z7)):
        up, down = add(u, shift(up, "z", ZS, 1)), add(d, shift(down, "z", ZS, 7))
    aggregate = add(z0, shift(up, "z", ZS, 1), shift(down, "z", ZS, 7))
    input_grad = jnp.einsum("qfj,df->qjd", aggregate, weight, preferred_element_type=F32)
    input_grad = input_grad.astype(BF16).reshape(features.shape[0], weight.shape[0])

    grad = grad + lax.ppermute(grad, "core", [(0, 1), (1, 0)])
    grad = grad + shift(grad, "y", YS, 1) + shift(grad, "y", YS, 3) + shift(grad, "y", YS, 2)
    grad = grad + shift(grad, "x", XS, 1) + shift(grad, "x", XS, 3) + shift(grad, "x", XS, 2)
    grad = grad + shift(grad, "z", ZS, 1) + shift(grad, "z", ZS, 7) + shift(grad, "z", ZS, 2)
    grad = grad + shift(grad, "z", ZS, 4)
    return input_grad, importance - grad.T * weight_delta


def solution(mesh):
    mesh = Mesh(mesh.devices.reshape(XS, ZS, YS, CS), ("x", "z", "y", "core"))
    row, col = ("x", "z"), ("y", "core")
    return jax.shard_map(
        local,
        mesh=mesh,
        in_specs=(
            P(row, col, None, None, None),
            P(row, col, None),
            P(row, col, None),
            P(row, col),
            P(row, col),
            P(row, col),
            P(row + col, None),
            P(),
            P(),
            P(),
        ),
        out_specs=(P(row + col, None), P()),
        check_vma=False,
    )
```

```python
import jax
import jax.numpy as jnp
from jax import lax
from jax.experimental import pallas as pl
from jax.experimental.pallas import tpu as pltpu
from jax.sharding import Mesh, PartitionSpec as P

XS, ZS, YS, CS = 4, 8, 4, 2
T = 128
UNROLL = 8
F32, BF16 = jnp.float32, jnp.bfloat16


def shift(value, axis, size, by):
    return lax.ppermute(value, axis, [(i, (i + by) % size) for i in range(size)])


def fetch_kernel(source, target, sem):
    copy = pltpu.make_async_copy(source, target, sem)
    copy.start()
    copy.wait()


def fetch(array):
    return pl.pallas_call(
        fetch_kernel,
        in_specs=[pl.BlockSpec(memory_space=pl.ANY)],
        out_specs=pl.BlockSpec(memory_space=pltpu.VMEM),
        out_shape=jax.ShapeDtypeStruct(array.shape, array.dtype),
        scratch_shapes=[pltpu.SemaphoreType.DMA],
        compiler_params=pltpu.CompilerParams(vmem_limit_bytes=12 * 2**20),
        cost_estimate=pl.CostEstimate(flops=0, bytes_accessed=16 * 2**20, transcendentals=0),
    )(array)


PLACED = ((64, 16), (80, 16), (48, 16), (96, 16), (32, 16), (112, 16), (0, 32))


def tile_kernel(rows, places, meta, tiles, mine, other, *rest):
    outs, (wide, acc) = rest[:7], rest[7:]
    for part, dist in enumerate((0, 1, 3, 2)):
        y_of = (meta[1] - dist) & (YS - 1)
        for ref, core in ((mine, meta[2]), (other, 1 - meta[2])):
            at = pl.multiple_of((y_of * CS + core) * 16, 16)
            wide[pl.ds(at, 16), :] = ref[part * 16 : part * 16 + 16, :]

    def clear(i, _):
        acc[pl.ds(i * 4, 4)] = jnp.zeros((4, T, T), F32)
        return 0

    lax.fori_loop(0, 32, clear, 0)

    def several(g, _):
        base = g * UNROLL
        products = []
        for u in range(UNROLL):
            at = pl.multiple_of(rows[base + u] * T, T)
            products.append(jnp.dot(wide[:, pl.ds(at, T)], tiles[base + u], preferred_element_type=F32))
        for u in range(UNROLL):
            place = places[base + u]
            acc[place] = acc[place] + products[u]
        return 0

    used = jnp.clip(meta[0], 0, tiles.shape[0])
    lax.fori_loop(0, (used + UNROLL - 1) >> 3, several, 0)

    for out, (first, size) in zip(outs, PLACED):

        def put(i, _):
            out[pl.ds(i * 4, 4)] = acc[pl.ds(first + i * 4, 4)].astype(BF16)
            return 0

        lax.fori_loop(0, size // 4, put, 0)


def tile_products(rows, places, meta, tiles, mine, other):
    smem, vmem = pl.BlockSpec(memory_space=pltpu.SMEM), pl.BlockSpec(memory_space=pltpu.VMEM)
    return pl.pallas_call(
        tile_kernel,
        in_specs=[smem] * 3 + [vmem] * 3,
        out_specs=[vmem] * 7,
        scratch_shapes=[pltpu.VMEM((T, mine.shape[1]), BF16), pltpu.VMEM((129, T, T), F32)],
        out_shape=[jax.ShapeDtypeStruct((n, T, T), BF16) for _, n in PLACED],
        compiler_params=pltpu.CompilerParams(vmem_limit_bytes=32 * 2**20),
        cost_estimate=pl.CostEstimate(flops=2**30, bytes_accessed=13 * 2**20, transcendentals=0),
    )(rows, places, meta, tiles, mine, other)


def middle_kernel(c0, upa, upb, downa, downb, feats, out, grad):
    grad[...] = jnp.zeros((T, T), F32)
    for first, up, down in ((0, upa, downa), (16, upb, downb)):

        def several(i, _):
            total = grad[...]
            for u in range(4):
                n, k = i * 4 + u, first + i * 4 + u
                value = (c0[k].astype(F32) + up[n].astype(F32) + down[n].astype(F32)).astype(BF16)
                out[k] = value
                total += jnp.dot(value, feats[k], preferred_element_type=F32)
            grad[...] = total
            return 0

        lax.fori_loop(0, 4, several, 0)


def middle(*operands):
    spec = pl.BlockSpec(memory_space=pltpu.VMEM)
    return pl.pallas_call(
        middle_kernel,
        in_specs=[spec] * 6,
        out_specs=[spec] * 2,
        out_shape=[jax.ShapeDtypeStruct((32, T, T), BF16), jax.ShapeDtypeStruct((T, T), F32)],
        compiler_params=pltpu.CompilerParams(vmem_limit_bytes=12 * 2**20),
        cost_estimate=pl.CostEstimate(flops=2**27, bytes_accessed=5 * 2**20, transcendentals=0),
    )(*operands)


def add(*values):
    return sum(v.astype(F32) for v in values).astype(BF16)


def local(tile_vals, tile_row, tile_col, tile_count, out_grad, relu_mask, features, weight, importance, weight_delta):
    x, y, core = (lax.axis_index(a) for a in ("x", "y", "core"))
    slots = tile_vals.shape[2]
    wide_feats = lax.all_gather(features, "z", axis=0, tiled=True).reshape(ZS * 4, T, T)

    masked = (out_grad.astype(F32) * relu_mask.astype(F32)).astype(BF16).T
    mine = jnp.concatenate([masked] + [shift(masked, "y", YS, d) for d in (1, 3, 2)], axis=0)
    other = lax.ppermute(mine, "core", [(0, 1), (1, 0)])

    count = tile_count.reshape(())
    cols = tile_col.reshape(slots)
    dest = cols >> 2
    dx = ((dest >> 3) - x) & (XS - 1)
    places = jnp.where(lax.iota(jnp.int32, slots) < count, dx * 32 + (cols & 31), 128)
    meta = jnp.stack([count, y, core]).astype(jnp.int32)
    tiles = fetch(tile_vals.reshape(slots, T, T))
    c2a, c2b, c1b, c3a, c1a, c3b, c0 = tile_products(tile_row.reshape(slots), places, meta, tiles, mine, other)

    up, down = shift(c2a, "x", XS, 1), shift(c2b, "x", XS, 3)
    upb, downa = shift(c1b, "x", XS, 1), shift(c3a, "x", XS, 3)
    upa, downb = shift(add(c1a, up), "x", XS, 1), shift(add(c3b, down), "x", XS, 3)
    reduced, grad = middle(c0, upa, upb, downa, downb, wide_feats)

    aggregate = lax.psum_scatter(reduced, "z", scatter_dimension=0, tiled=True)
    input_grad = jnp.einsum("qfj,df->qjd", aggregate, weight, preferred_element_type=F32)
    input_grad = input_grad.astype(BF16).reshape(features.shape[0], weight.shape[0])

    grad = grad + lax.ppermute(grad, "core", [(0, 1), (1, 0)])
    grad = grad + shift(grad, "y", YS, 1) + shift(grad, "y", YS, 3) + shift(grad, "y", YS, 2)
    grad = grad + shift(grad, "x", XS, 1) + shift(grad, "x", XS, 3) + shift(grad, "x", XS, 2)
    grad = grad + shift(grad, "z", ZS, 1) + shift(grad, "z", ZS, 7) + shift(grad, "z", ZS, 2)
    grad = grad + shift(grad, "z", ZS, 4)
    return input_grad, importance - grad.T * weight_delta


def solution(mesh):
    mesh = Mesh(mesh.devices.reshape(XS, ZS, YS, CS), ("x", "z", "y", "core"))
    row, col = ("x", "z"), ("y", "core")
    return jax.shard_map(
        local,
        mesh=mesh,
        in_specs=(
            P(row, col, None, None, None),
            P(row, col, None),
            P(row, col, None),
            P(row, col),
            P(row, col),
            P(row, col),
            P(row + col, None),
            P(),
            P(),
            P(),
        ),
        out_specs=(P(row + col, None), P()),
        check_vma=False,
    )
```

```python
import jax
import jax.numpy as jnp
from jax import lax
from jax.experimental import pallas as pl
from jax.experimental.pallas import tpu as pltpu
from jax.sharding import Mesh, PartitionSpec as P

XS, ZS, YS, CS = 4, 8, 4, 2
T = 128
GROUP = 32
F32, BF16 = jnp.float32, jnp.bfloat16


def shift(value, axis, size, by):
    return lax.ppermute(value, axis, [(i, (i + by) % size) for i in range(size)])


def swap(value):
    return lax.ppermute(value, "core", [(0, 1), (1, 0)])


def spread(value, axis, size, dists, core):
    total = jnp.where(core == 0, value, jnp.zeros_like(value))
    for by in dists:
        pairs = [
            (i * CS + c, (i + d) % size * CS + c) for c, d in enumerate(by) if d is not None for i in range(size)
        ]
        total = total + lax.ppermute(value, (axis, "core"), pairs)
    return total


def fetch_kernel(source, target, sem):
    copy = pltpu.make_async_copy(source, target, sem)
    copy.start()
    copy.wait()


def fetch(array):
    return pl.pallas_call(
        fetch_kernel,
        in_specs=[pl.BlockSpec(memory_space=pl.ANY)],
        out_specs=pl.BlockSpec(memory_space=pltpu.VMEM),
        out_shape=jax.ShapeDtypeStruct(array.shape, array.dtype),
        scratch_shapes=[pltpu.SemaphoreType.DMA],
        compiler_params=pltpu.CompilerParams(vmem_limit_bytes=12 * 2**20),
        cost_estimate=pl.CostEstimate(flops=0, bytes_accessed=2 * array.size, transcendentals=0),
    )(array)


DISTS = (2, 1, 3)
PLACED = ((64, 16), (80, 16), (48, 16), (96, 16), (32, 16), (112, 16), (0, 32))


def tile_kernel(codes, meta, source, mine, other, *rest):
    outs, (tiles, wide, acc, sems) = rest[:7], rest[7:]
    steps = source.shape[0] // GROUP

    def chunk(g):
        at = pl.ds(pl.multiple_of(g * GROUP, GROUP), GROUP)
        return pltpu.make_async_copy(source.at[at], tiles.at[at], sems.at[g])

    for g in range(steps):
        chunk(g).start()
    for part, dist in enumerate((0,) + DISTS):
        y_of = (meta[1] - dist) & (YS - 1)
        for ref, core in ((mine, meta[2]), (other, 1 - meta[2])):
            at = pl.multiple_of((y_of * CS + core) * 16, 16)
            wide[pl.ds(at, 16), :] = ref[part * 16 : part * 16 + 16, :]

    def clear(i, _):
        acc[pl.ds(i * 4, 4)] = jnp.zeros((4, T, T), F32)
        return 0

    lax.fori_loop(0, 32, clear, 0)

    def several(g, _):
        chunk(g).wait()

        @pl.when(g * GROUP < meta[0])
        def _():
            base = g * GROUP
            products = []
            for u in range(GROUP):
                at = pl.multiple_of((codes[base + u] >> 8) * T, T)
                products.append(
                    jnp.dot(wide[:, pl.ds(at, T)], tiles[base + u], preferred_element_type=F32)
                )
            for u in range(GROUP):
                place = codes[base + u] & 255
                acc[place] = acc[place] + products[u]

        return 0

    lax.fori_loop(0, steps, several, 0)

    for out, (first, size) in zip(outs, PLACED):

        def put(i, _):
            out[pl.ds(i * 4, 4)] = acc[pl.ds(first + i * 4, 4)].astype(BF16)
            return 0

        lax.fori_loop(0, size // 4, put, 0)


def tile_products(codes, meta, tiles, mine, other):
    smem, vmem = pl.BlockSpec(memory_space=pltpu.SMEM), pl.BlockSpec(memory_space=pltpu.VMEM)
    return pl.pallas_call(
        tile_kernel,
        in_specs=[smem] * 2 + [pl.BlockSpec(memory_space=pl.ANY)] + [vmem] * 2,
        out_specs=[vmem] * 7,
        scratch_shapes=[
            pltpu.VMEM(tiles.shape, BF16),
            pltpu.VMEM((T, mine.shape[1]), BF16),
            pltpu.VMEM((129, T, T), F32),
            pltpu.SemaphoreType.DMA((tiles.shape[0] // GROUP,)),
        ],
        out_shape=[jax.ShapeDtypeStruct((n, T, T), BF16) for _, n in PLACED],
        compiler_params=pltpu.CompilerParams(vmem_limit_bytes=50 * 2**20),
        cost_estimate=pl.CostEstimate(flops=2**30, bytes_accessed=13 * 2**20, transcendentals=0),
    )(codes, meta, tiles, mine, other)


def middle_kernel(c0, upa, upb, downa, downb, feats, out, grad, sums):
    sums[...] = jnp.zeros((T, T), F32)
    for first, up, down in ((0, upa, downa), (16, upb, downb)):

        def several(i, _):
            total = sums[...]
            for u in range(4):
                n, k = i * 4 + u, first + i * 4 + u
                value = (c0[k].astype(F32) + up[n].astype(F32) + down[n].astype(F32)).astype(BF16)
                out[k] = value
                total += jnp.dot(value, feats[k], preferred_element_type=F32)
            sums[...] = total
            return 0

        lax.fori_loop(0, 4, several, 0)
    grad[...] = sums[...].T


def middle(*operands):
    spec = pl.BlockSpec(memory_space=pltpu.VMEM)
    return pl.pallas_call(
        middle_kernel,
        in_specs=[spec] * 6,
        out_specs=[spec] * 2,
        out_shape=[jax.ShapeDtypeStruct((32, T, T), BF16), jax.ShapeDtypeStruct((T, T), F32)],
        scratch_shapes=[pltpu.VMEM((T, T), F32)],
        compiler_params=pltpu.CompilerParams(vmem_limit_bytes=12 * 2**20),
        cost_estimate=pl.CostEstimate(flops=2**27, bytes_accessed=5 * 2**20, transcendentals=0),
    )(*operands)


def last_kernel(aggregate, weight, grad, more, importance, delta, input_grad, importance_out):
    for q in range(4):
        product = jnp.dot(weight[...], aggregate[q], preferred_element_type=F32)
        input_grad[q * T : q * T + T, :] = product.T.astype(BF16)
    importance_out[...] = importance[...] - (grad[...] + more[...]) * delta[...]


def last(*operands):
    spec = pl.BlockSpec(memory_space=pltpu.VMEM)
    return pl.pallas_call(
        last_kernel,
        in_specs=[spec] * 6,
        out_specs=[spec] * 2,
        out_shape=[jax.ShapeDtypeStruct((4 * T, T), BF16), jax.ShapeDtypeStruct((T, T), F32)],
        compiler_params=pltpu.CompilerParams(vmem_limit_bytes=4 * 2**20),
        cost_estimate=pl.CostEstimate(flops=2**24, bytes_accessed=2**19, transcendentals=0),
    )(*operands)


def add(*values):
    return sum(v.astype(F32) for v in values).astype(BF16)


def local(tile_vals, tile_row, tile_col, tile_count, out_grad, relu_mask, features, weight, importance, weight_delta):
    x, y, core = (lax.axis_index(a) for a in ("x", "y", "core"))
    slots = tile_vals.shape[2]
    wide_feats = lax.all_gather(features, "z", axis=0, tiled=True).reshape(ZS * 4, T, T)

    masked = (out_grad.astype(F32) * relu_mask.astype(F32)).astype(BF16).T
    mine = jnp.concatenate([masked] + [shift(masked, "y", YS, d) for d in DISTS], axis=0)
    other = swap(mine)

    count = tile_count.reshape(())
    cols = tile_col.reshape(slots)
    dest = cols >> 2
    dx = ((dest >> 3) - x) & (XS - 1)
    places = jnp.where(lax.iota(jnp.int32, slots) < count, dx * 32 + (cols & 31), 128)
    codes = tile_row.reshape(slots) * 256 + places
    meta = jnp.stack([count, y, core]).astype(jnp.int32)
    tiles = tile_vals.reshape(slots, T, T)
    c2a, c2b, c1b, c3a, c1a, c3b, c0 = tile_products(codes, meta, tiles, mine, other)

    up, down = shift(c2a, "x", XS, 1), shift(c2b, "x", XS, 3)
    upb, downa = shift(c1b, "x", XS, 1), shift(c3a, "x", XS, 3)
    upa, downb = shift(add(c1a, up), "x", XS, 1), shift(add(c3b, down), "x", XS, 3)
    reduced, grad = middle(c0, upa, upb, downa, downb, fetch(wide_feats))

    aggregate = lax.psum_scatter(reduced, "z", scatter_dimension=0, tiled=True)

    grad = grad + swap(grad)
    grad = grad + shift(grad, "y", YS, 2) + shift(grad, "y", YS, 1) + shift(grad, "y", YS, 3)
    grad = grad + shift(grad, "x", XS, 2) + shift(grad, "x", XS, 1) + shift(grad, "x", XS, 3)
    grad = spread(grad, "z", ZS, ((4, None), (3, 5), (2, 6), (1, 7)), core)
    return last(aggregate, weight, grad, swap(grad), importance, weight_delta)


def solution(mesh):
    mesh = Mesh(mesh.devices.reshape(XS, ZS, YS, CS), ("x", "z", "y", "core"))
    row, col = ("x", "z"), ("y", "core")
    return jax.shard_map(
        local,
        mesh=mesh,
        in_specs=(
            P(row, col, None, None, None),
            P(row, col, None),
            P(row, col, None),
            P(row, col),
            P(row, col),
            P(row, col),
            P(row + col, None),
            P(),
            P(),
            P(),
        ),
        out_specs=(P(row + col, None), P()),
        check_vma=False,
    )
```

```python
import functools

import jax
import jax.numpy as jnp
from jax import lax
from jax.experimental import pallas as pl
from jax.experimental.pallas import tpu as pltpu
from jax.sharding import Mesh, PartitionSpec as P

XS, ZS, YS, CS = 4, 8, 4, 2
T = 128
GROUP = 32
F32, BF16 = jnp.float32, jnp.bfloat16


def shift(value, axis, size, by):
    return lax.ppermute(value, axis, [(i, (i + by) % size) for i in range(size)])


def swap(value):
    return lax.ppermute(value, "core", [(0, 1), (1, 0)])


def spread(value, axis, size, dists, core):
    total = jnp.where(core == 0, value, jnp.zeros_like(value))
    for by in dists:
        pairs = [
            (i * CS + c, (i + d) % size * CS + c) for c, d in enumerate(by) if d is not None for i in range(size)
        ]
        total = total + lax.ppermute(value, (axis, "core"), pairs)
    return total


def fetch_kernel(source, target, sem):
    copy = pltpu.make_async_copy(source, target, sem)
    copy.start()
    copy.wait()


def fetch(array):
    return pl.pallas_call(
        fetch_kernel,
        in_specs=[pl.BlockSpec(memory_space=pl.ANY)],
        out_specs=pl.BlockSpec(memory_space=pltpu.VMEM),
        out_shape=jax.ShapeDtypeStruct(array.shape, array.dtype),
        scratch_shapes=[pltpu.SemaphoreType.DMA],
        compiler_params=pltpu.CompilerParams(vmem_limit_bytes=12 * 2**20),
        cost_estimate=pl.CostEstimate(flops=0, bytes_accessed=2 * array.size, transcendentals=0),
    )(array)


DISTS = (2, 1, 3)
CHUNK2 = ((64, 16), (80, 16))
OTHERS = ((48, 16), (96, 16), (32, 16), (112, 16), (0, 32))
UNUSED = 128


def sort_kernel(rows, cols, count, x, lists):
    slots = rows.shape[0]
    second = slots + GROUP

    def some(i, found):
        a, b = found
        for u in range(4):
            t = i * 4 + u
            col = cols[t]
            dx = ((col >> 5) - x[0]) & (XS - 1)
            entry = t * 8192 + rows[t] * 256 + dx * 32 + (col & 31)
            lists[a] = entry
            lists[b] = entry
            used = jnp.where(t < count[0], 1, 0)
            is_first = jnp.where(dx == 2, used, 0)
            a = a + is_first
            b = b + (used - is_first)
        return a, b

    a, b = lax.fori_loop(0, slots // 4, some, (jnp.int32(0), jnp.int32(second)))

    def fill(i, _):
        lists[a + i] = UNUSED
        lists[b + i] = UNUSED
        return 0

    lax.fori_loop(0, GROUP, fill, 0)
    lists[2 * second] = a
    lists[2 * second + 1] = b - second


def sort_tiles(*operands):
    smem = pl.BlockSpec(memory_space=pltpu.SMEM)
    return pl.pallas_call(
        sort_kernel,
        in_specs=[smem] * 4,
        out_specs=smem,
        out_shape=jax.ShapeDtypeStruct((2 * (operands[0].shape[0] + GROUP) + 2,), jnp.int32),
        cost_estimate=pl.CostEstimate(flops=0, bytes_accessed=2**12, transcendentals=0),
    )(*operands)


def join_kernel(token, *refs):
    for i, ref in enumerate(refs[:-1]):
        refs[-1][i * 16 : i * 16 + 16, :] = ref[...]


def join(token, *parts):
    spec = pl.BlockSpec(memory_space=pltpu.VMEM)
    return pl.pallas_call(
        join_kernel,
        in_specs=[pl.BlockSpec(memory_space=pltpu.SMEM)] + [spec] * len(parts),
        out_specs=spec,
        out_shape=jax.ShapeDtypeStruct((16 * len(parts), parts[0].shape[1]), BF16),
        compiler_params=pltpu.CompilerParams(vmem_limit_bytes=4 * 2**20),
        cost_estimate=pl.CostEstimate(flops=0, bytes_accessed=2**18, transcendentals=0),
    )(token, *parts)


def tile_kernel(which, placed, codes, meta, source, mine, other, *rest):
    outs, (tiles, wide, acc, sems) = rest[: len(placed)], rest[len(placed) :]
    slots = source.shape[0]
    start = which * (slots + GROUP)
    groups = (codes[2 * (slots + GROUP) + which] + GROUP - 1) >> 5

    def bring(g, _):
        for u in range(GROUP):
            n = g * GROUP + u
            pltpu.make_async_copy(source.at[codes[start + n] >> 13], tiles.at[n], sems.at[g]).start()
        return 0

    lax.fori_loop(0, groups, bring, 0)
    for part, dist in enumerate((0,) + DISTS):
        y_of = (meta[0] - dist) & (YS - 1)
        for ref, core in ((mine, meta[1]), (other, 1 - meta[1])):
            at = pl.multiple_of((y_of * CS + core) * 16, 16)
            wide[pl.ds(at, 16), :] = ref[part * 16 : part * 16 + 16, :]
    for first, size in placed:

        def clear(i, _):
            acc[pl.ds(first + i * 4, 4)] = jnp.zeros((4, T, T), F32)
            return 0

        lax.fori_loop(0, size // 4, clear, 0)

    def several(g, _):
        base = pl.multiple_of(g * GROUP, GROUP)
        here = tiles.at[pl.ds(base, GROUP)]
        pltpu.make_async_copy(source.at[pl.ds(0, GROUP)], here, sems.at[g]).wait()
        products = []
        for u in range(GROUP):
            at = pl.multiple_of(((codes[start + base + u] >> 8) & 31) * T, T)
            products.append(jnp.dot(wide[:, pl.ds(at, T)], tiles[base + u], preferred_element_type=F32))
        for u in range(GROUP):
            place = codes[start + base + u] & 255
            acc[place] = acc[place] + products[u]
        return 0

    lax.fori_loop(0, groups, several, 0)

    for out, (first, size) in zip(outs, placed):

        def put(i, _):
            out[pl.ds(i * 4, 4)] = acc[pl.ds(first + i * 4, 4)].astype(BF16)
            return 0

        lax.fori_loop(0, size // 4, put, 0)


def tile_products(which, placed, codes, meta, tiles, mine, other):
    smem, vmem = pl.BlockSpec(memory_space=pltpu.SMEM), pl.BlockSpec(memory_space=pltpu.VMEM)
    return pl.pallas_call(
        functools.partial(tile_kernel, which, placed),
        in_specs=[smem] * 2 + [pl.BlockSpec(memory_space=pl.ANY)] + [vmem] * 2,
        out_specs=[vmem] * len(placed),
        scratch_shapes=[
            pltpu.VMEM(tiles.shape, BF16),
            pltpu.VMEM((T, mine.shape[1]), BF16),
            pltpu.VMEM((129, T, T), F32),
            pltpu.SemaphoreType.DMA((tiles.shape[0] // GROUP,)),
        ],
        out_shape=[jax.ShapeDtypeStruct((n, T, T), BF16) for _, n in placed],
        compiler_params=pltpu.CompilerParams(vmem_limit_bytes=46 * 2**20),
        cost_estimate=pl.CostEstimate(flops=0, bytes_accessed=2**24, transcendentals=0),
    )(codes, meta, tiles, mine, other)


def middle_kernel(c0, upa, upb, downa, downb, feats, out, grad):
    total = jnp.zeros((T, T), F32)
    for k in range(32):
        up, down = (upa, downa) if k < 16 else (upb, downb)
        n = k % 16
        value = (c0[k].astype(F32) + up[n].astype(F32) + down[n].astype(F32)).astype(BF16)
        out[k] = value
        total += jnp.dot(value, feats[k], preferred_element_type=F32)
    grad[...] = total.T


def middle(*operands):
    spec = pl.BlockSpec(memory_space=pltpu.VMEM)
    return pl.pallas_call(
        middle_kernel,
        in_specs=[spec] * 6,
        out_specs=[spec] * 2,
        out_shape=[jax.ShapeDtypeStruct((32, T, T), BF16), jax.ShapeDtypeStruct((T, T), F32)],
        compiler_params=pltpu.CompilerParams(vmem_limit_bytes=12 * 2**20),
        cost_estimate=pl.CostEstimate(flops=2**27, bytes_accessed=5 * 2**20, transcendentals=0),
    )(*operands)


def last_kernel(aggregate, weight, grad, more, importance, delta, input_grad, importance_out):
    for q in range(4):
        product = jnp.dot(weight[...], aggregate[q], preferred_element_type=F32)
        input_grad[q * T : q * T + T, :] = product.T.astype(BF16)
    importance_out[...] = importance[...] - (grad[...] + more[...]) * delta[...]


def last(*operands):
    spec = pl.BlockSpec(memory_space=pltpu.VMEM)
    return pl.pallas_call(
        last_kernel,
        in_specs=[spec] * 6,
        out_specs=[spec] * 2,
        out_shape=[jax.ShapeDtypeStruct((4 * T, T), BF16), jax.ShapeDtypeStruct((T, T), F32)],
        compiler_params=pltpu.CompilerParams(vmem_limit_bytes=4 * 2**20),
        cost_estimate=pl.CostEstimate(flops=2**24, bytes_accessed=2**19, transcendentals=0),
    )(*operands)


def add(*values):
    return sum(v.astype(F32) for v in values).astype(BF16)


def local(tile_vals, tile_row, tile_col, tile_count, out_grad, relu_mask, features, weight, importance, weight_delta):
    x, y, core = (lax.axis_index(a) for a in ("x", "y", "core"))
    slots = tile_vals.shape[2]
    wide_feats = lax.all_gather(features, "z", axis=0, tiled=True).reshape(ZS * 4, T, T)

    masked = (out_grad.astype(F32) * relu_mask.astype(F32)).astype(BF16).T
    codes = sort_tiles(tile_row.reshape(slots), tile_col.reshape(slots), tile_count.reshape(1), x.reshape(1))
    meta = jnp.stack([y, core]).astype(jnp.int32)

    mine = join(codes, masked, *(shift(masked, "y", YS, d) for d in DISTS))
    operands = (codes, meta, tile_vals.reshape(slots, T, T), mine, swap(mine))
    c2a, c2b = tile_products(0, CHUNK2, *operands)
    c1b, c3a, c1a, c3b, c0 = tile_products(1, OTHERS, *operands)

    up, down = shift(c2a, "x", XS, 1), shift(c2b, "x", XS, 3)
    upb, downa = shift(c1b, "x", XS, 1), shift(c3a, "x", XS, 3)
    upa, downb = shift(add(c1a, up), "x", XS, 1), shift(add(c3b, down), "x", XS, 3)
    reduced, grad = middle(fetch(c0), upa, upb, downa, downb, fetch(wide_feats))

    aggregate = lax.psum_scatter(reduced, "z", scatter_dimension=0, tiled=True)

    grad = grad + swap(grad)
    grad = grad + shift(grad, "y", YS, 2) + shift(grad, "y", YS, 1) + shift(grad, "y", YS, 3)
    grad = grad + shift(grad, "x", XS, 2) + shift(grad, "x", XS, 1) + shift(grad, "x", XS, 3)
    grad = spread(grad, "z", ZS, ((4, None), (3, 5), (2, 6), (1, 7)), core)
    return last(aggregate, weight, grad, swap(grad), importance, weight_delta)


def solution(mesh):
    mesh = Mesh(mesh.devices.reshape(XS, ZS, YS, CS), ("x", "z", "y", "core"))
    row, col = ("x", "z"), ("y", "core")
    return jax.shard_map(
        local,
        mesh=mesh,
        in_specs=(
            P(row, col, None, None, None),
            P(row, col, None),
            P(row, col, None),
            P(row, col),
            P(row, col),
            P(row, col),
            P(row + col, None),
            P(),
            P(),
            P(),
        ),
        out_specs=(P(row + col, None), P()),
        check_vma=False,
    )
```

```python
import functools

import jax
import jax.numpy as jnp
from jax import lax
from jax.experimental import pallas as pl
from jax.experimental.pallas import tpu as pltpu
from jax.sharding import Mesh, PartitionSpec as P

XS, ZS, YS, CS = 4, 8, 4, 2
T = 128
GROUP = 32
F32, BF16 = jnp.float32, jnp.bfloat16


def shift(value, axis, size, by):
    return lax.ppermute(value, axis, [(i, (i + by) % size) for i in range(size)])


def swap(value):
    return lax.ppermute(value, "core", [(0, 1), (1, 0)])


def spread(value, axis, size, dists, core):
    total = jnp.where(core == 0, value, jnp.zeros_like(value))
    for by in dists:
        pairs = [
            (i * CS + c, (i + d) % size * CS + c) for c, d in enumerate(by) if d is not None for i in range(size)
        ]
        total = total + lax.ppermute(value, (axis, "core"), pairs)
    return total


def fetch_kernel(source, target, sem):
    copy = pltpu.make_async_copy(source, target, sem)
    copy.start()
    copy.wait()


def fetch(array):
    return pl.pallas_call(
        fetch_kernel,
        in_specs=[pl.BlockSpec(memory_space=pl.ANY)],
        out_specs=pl.BlockSpec(memory_space=pltpu.VMEM),
        out_shape=jax.ShapeDtypeStruct(array.shape, array.dtype),
        scratch_shapes=[pltpu.SemaphoreType.DMA],
        compiler_params=pltpu.CompilerParams(vmem_limit_bytes=12 * 2**20),
        cost_estimate=pl.CostEstimate(flops=0, bytes_accessed=2 * array.size, transcendentals=0),
    )(array)


DISTS = (2, 1, 3)
CHUNK2 = ((64, 16), (80, 16))
OTHERS = ((48, 16), (96, 16), (32, 16), (112, 16), (0, 32))
UNUSED = 128
LISTS = 1024


def sort_kernel(rows, cols, count, x, out, lists, sem):
    slots = rows.shape[0]
    second = slots + GROUP

    def some(i, found):
        a, b = found
        for u in range(4):
            t = i * 4 + u
            col = cols[t]
            dx = ((col >> 5) - x[0]) & (XS - 1)
            entry = t * 8192 + rows[t] * 256 + dx * 32 + (col & 31)
            lists[a] = entry
            lists[b] = entry
            used = jnp.where(t < count[0], 1, 0)
            is_first = jnp.where(dx == 2, used, 0)
            a = a + is_first
            b = b + (used - is_first)
        return a, b

    a, b = lax.fori_loop(0, slots // 4, some, (jnp.int32(0), jnp.int32(second)))

    def fill(i, _):
        lists[a + i] = UNUSED
        lists[b + i] = UNUSED
        return 0

    lax.fori_loop(0, GROUP, fill, 0)
    lists[2 * second] = a
    lists[2 * second + 1] = b - second
    copy = pltpu.make_async_copy(lists, out.at[pl.ds(0, LISTS)], sem)
    copy.start()
    copy.wait()


def sort_tiles(*operands):
    smem = pl.BlockSpec(memory_space=pltpu.SMEM)
    return pl.pallas_call(
        sort_kernel,
        in_specs=[smem] * 4,
        out_specs=pl.BlockSpec(memory_space=pl.ANY),
        out_shape=jax.ShapeDtypeStruct((2**24,), jnp.int32),
        scratch_shapes=[pltpu.SMEM((LISTS,), jnp.int32), pltpu.SemaphoreType.DMA],
        cost_estimate=pl.CostEstimate(flops=0, bytes_accessed=2**12, transcendentals=0),
    )(*operands)


def join_kernel(token, *refs):
    for i, ref in enumerate(refs[:-1]):
        refs[-1][i * 16 : i * 16 + 16, :] = ref[...]


def join(token, *parts):
    spec = pl.BlockSpec(memory_space=pltpu.VMEM)
    return pl.pallas_call(
        join_kernel,
        in_specs=[pl.BlockSpec(memory_space=pl.ANY)] + [spec] * len(parts),
        out_specs=spec,
        out_shape=jax.ShapeDtypeStruct((16 * len(parts), parts[0].shape[1]), BF16),
        compiler_params=pltpu.CompilerParams(vmem_limit_bytes=4 * 2**20),
        cost_estimate=pl.CostEstimate(flops=0, bytes_accessed=2**18, transcendentals=0),
    )(token, *parts)


def tile_kernel(which, placed, lists, meta, source, mine, other, *rest):
    outs, (codes, tiles, wide, acc, list_sem, sems) = rest[: len(placed)], rest[len(placed) :]
    listed = pltpu.make_async_copy(lists.at[pl.ds(0, LISTS)], codes, list_sem)
    listed.start()
    for part, dist in enumerate((0,) + DISTS):
        y_of = (meta[0] - dist) & (YS - 1)
        for ref, core in ((mine, meta[1]), (other, 1 - meta[1])):
            at = pl.multiple_of((y_of * CS + core) * 16, 16)
            wide[pl.ds(at, 16), :] = ref[part * 16 : part * 16 + 16, :]
    listed.wait()
    slots = source.shape[0]
    start = which * (slots + GROUP)
    groups = (codes[2 * (slots + GROUP) + which] + GROUP - 1) >> 5

    def bring(g, _):
        for u in range(GROUP):
            n = g * GROUP + u
            pltpu.make_async_copy(source.at[codes[start + n] >> 13], tiles.at[n], sems.at[g]).start()
        return 0

    lax.fori_loop(0, groups, bring, 0)
    for first, size in placed:

        def clear(i, _):
            acc[pl.ds(first + i * 4, 4)] = jnp.zeros((4, T, T), F32)
            return 0

        lax.fori_loop(0, size // 4, clear, 0)

    def several(g, _):
        base = pl.multiple_of(g * GROUP, GROUP)
        here = tiles.at[pl.ds(base, GROUP)]
        pltpu.make_async_copy(source.at[pl.ds(0, GROUP)], here, sems.at[g]).wait()
        products = []
        for u in range(GROUP):
            at = pl.multiple_of(((codes[start + base + u] >> 8) & 31) * T, T)
            products.append(jnp.dot(wide[:, pl.ds(at, T)], tiles[base + u], preferred_element_type=F32))
        for u in range(GROUP):
            place = codes[start + base + u] & 255
            acc[place] = acc[place] + products[u]
        return 0

    lax.fori_loop(0, groups, several, 0)

    for out, (first, size) in zip(outs, placed):

        def put(i, _):
            out[pl.ds(i * 4, 4)] = acc[pl.ds(first + i * 4, 4)].astype(BF16)
            return 0

        lax.fori_loop(0, size // 4, put, 0)


def tile_products(which, placed, codes, meta, tiles, mine, other):
    smem, vmem = pl.BlockSpec(memory_space=pltpu.SMEM), pl.BlockSpec(memory_space=pltpu.VMEM)
    return pl.pallas_call(
        functools.partial(tile_kernel, which, placed),
        in_specs=[pl.BlockSpec(memory_space=pl.ANY), smem, pl.BlockSpec(memory_space=pl.ANY)] + [vmem] * 2,
        out_specs=[vmem] * len(placed),
        scratch_shapes=[
            pltpu.SMEM((LISTS,), jnp.int32),
            pltpu.VMEM(tiles.shape, BF16),
            pltpu.VMEM((T, mine.shape[1]), BF16),
            pltpu.VMEM((129, T, T), F32),
            pltpu.SemaphoreType.DMA,
            pltpu.SemaphoreType.DMA((tiles.shape[0] // GROUP,)),
        ],
        out_shape=[jax.ShapeDtypeStruct((n, T, T), BF16) for _, n in placed],
        compiler_params=pltpu.CompilerParams(vmem_limit_bytes=46 * 2**20),
        cost_estimate=pl.CostEstimate(flops=0, bytes_accessed=2**24, transcendentals=0),
    )(codes, meta, tiles, mine, other)


def middle_kernel(c0, upa, upb, downa, downb, feats, out, grad):
    total = jnp.zeros((T, T), F32)
    for k in range(32):
        up, down = (upa, downa) if k < 16 else (upb, downb)
        n = k % 16
        value = (c0[k].astype(F32) + up[n].astype(F32) + down[n].astype(F32)).astype(BF16)
        out[k] = value
        total += jnp.dot(value, feats[k], preferred_element_type=F32)
    grad[...] = total.T


def middle(*operands):
    spec = pl.BlockSpec(memory_space=pltpu.VMEM)
    return pl.pallas_call(
        middle_kernel,
        in_specs=[spec] * 6,
        out_specs=[spec] * 2,
        out_shape=[jax.ShapeDtypeStruct((32, T, T), BF16), jax.ShapeDtypeStruct((T, T), F32)],
        compiler_params=pltpu.CompilerParams(vmem_limit_bytes=12 * 2**20),
        cost_estimate=pl.CostEstimate(flops=2**27, bytes_accessed=5 * 2**20, transcendentals=0),
    )(*operands)


def last_kernel(aggregate, weight, grad, more, importance, delta, input_grad, importance_out):
    importance_out[...] = importance[...] - (grad[...] + more[...]) * delta[...]
    for q in range(4):
        product = jnp.dot(weight[...], aggregate[q], preferred_element_type=F32)
        input_grad[q * T : q * T + T, :] = product.T.astype(BF16)


def last(*operands):
    spec = pl.BlockSpec(memory_space=pltpu.VMEM)
    return pl.pallas_call(
        last_kernel,
        in_specs=[spec] * 6,
        out_specs=[spec] * 2,
        out_shape=[jax.ShapeDtypeStruct((4 * T, T), BF16), jax.ShapeDtypeStruct((T, T), F32)],
        compiler_params=pltpu.CompilerParams(vmem_limit_bytes=4 * 2**20),
        cost_estimate=pl.CostEstimate(flops=2**24, bytes_accessed=2**19, transcendentals=0),
    )(*operands)


def add(*values):
    return sum(v.astype(F32) for v in values).astype(BF16)


def local(tile_vals, tile_row, tile_col, tile_count, out_grad, relu_mask, features, weight, importance, weight_delta):
    x, y, core = (lax.axis_index(a) for a in ("x", "y", "core"))
    slots = tile_vals.shape[2]
    wide_feats = lax.all_gather(features, "z", axis=0, tiled=True).reshape(ZS * 4, T, T)

    masked = (out_grad.astype(F32) * relu_mask.astype(F32)).astype(BF16).T
    codes = sort_tiles(tile_row.reshape(slots), tile_col.reshape(slots), tile_count.reshape(1), x.reshape(1))
    meta = jnp.stack([y, core]).astype(jnp.int32)

    mine = join(codes, masked, *(shift(masked, "y", YS, d) for d in DISTS))
    operands = (codes, meta, tile_vals.reshape(slots, T, T), mine, swap(mine))
    c2a, c2b = tile_products(0, CHUNK2, *operands)
    c1b, c3a, c1a, c3b, c0 = tile_products(1, OTHERS, *operands)

    up, down = shift(c2a, "x", XS, 1), shift(c2b, "x", XS, 3)
    upb, downa = shift(c1b, "x", XS, 1), shift(c3a, "x", XS, 3)
    upa, downb = shift(add(c1a, up), "x", XS, 1), shift(add(c3b, down), "x", XS, 3)
    reduced, grad = middle(fetch(c0), upa, upb, downa, downb, fetch(wide_feats))

    aggregate = lax.psum_scatter(reduced, "z", scatter_dimension=0, tiled=True)

    grad = grad + swap(grad)
    grad = grad + shift(grad, "y", YS, 2) + shift(grad, "y", YS, 1) + shift(grad, "y", YS, 3)
    grad = grad + shift(grad, "x", XS, 2) + shift(grad, "x", XS, 1) + shift(grad, "x", XS, 3)
    grad = spread(grad, "z", ZS, ((1, 7), (2, 6), (3, 5), (4, None)), core)
    return last(aggregate, weight, grad, swap(grad), importance, weight_delta)


def solution(mesh):
    mesh = Mesh(mesh.devices.reshape(XS, ZS, YS, CS), ("x", "z", "y", "core"))
    row, col = ("x", "z"), ("y", "core")
    return jax.shard_map(
        local,
        mesh=mesh,
        in_specs=(
            P(row, col, None, None, None),
            P(row, col, None),
            P(row, col, None),
            P(row, col),
            P(row, col),
            P(row, col),
            P(row + col, None),
            P(),
            P(),
            P(),
        ),
        out_specs=(P(row + col, None), P()),
        check_vma=False,
    )
```

```python
import functools

import jax
import jax.numpy as jnp
from jax import lax
from jax.experimental import pallas as pl
from jax.experimental.pallas import tpu as pltpu
from jax.sharding import Mesh, PartitionSpec as P

XS, ZS, YS, CS = 4, 8, 4, 2
T = 128
GROUP = 32
F32, BF16 = jnp.float32, jnp.bfloat16


def shift(value, axis, size, by):
    return lax.ppermute(value, axis, [(i, (i + by) % size) for i in range(size)])


def swap(value):
    return lax.ppermute(value, "core", [(0, 1), (1, 0)])


def spread(value, axis, size, dists, core):
    total = jnp.where(core == 0, value, jnp.zeros_like(value))
    for by in dists:
        pairs = [
            (i * CS + c, (i + d) % size * CS + c) for c, d in enumerate(by) if d is not None for i in range(size)
        ]
        total = total + lax.ppermute(value, (axis, "core"), pairs)
    return total


def fetch_kernel(source, target, sem):
    copy = pltpu.make_async_copy(source, target, sem)
    copy.start()
    copy.wait()


def fetch(array):
    return pl.pallas_call(
        fetch_kernel,
        in_specs=[pl.BlockSpec(memory_space=pl.ANY)],
        out_specs=pl.BlockSpec(memory_space=pltpu.VMEM),
        out_shape=jax.ShapeDtypeStruct(array.shape, array.dtype),
        scratch_shapes=[pltpu.SemaphoreType.DMA],
        compiler_params=pltpu.CompilerParams(vmem_limit_bytes=12 * 2**20),
        cost_estimate=pl.CostEstimate(flops=0, bytes_accessed=2 * array.size, transcendentals=0),
    )(array)


DISTS = (2, 1, 3)
CHUNK2 = ((64, 16), (80, 16))
OTHERS = ((48, 16), (96, 16), (32, 16), (112, 16), (0, 32))
UNUSED = 128
LISTS = 1024


def sort_kernel(rows, cols, count, x, out, lists, sem):
    slots = rows.shape[0]
    second = slots + GROUP

    def some(i, found):
        a, b = found
        for u in range(4):
            t = i * 4 + u
            col = cols[t]
            dx = ((col >> 5) - x[0]) & (XS - 1)
            entry = t * 8192 + rows[t] * 256 + dx * 32 + (col & 31)
            lists[a] = entry
            lists[b] = entry
            used = jnp.where(t < count[0], 1, 0)
            is_first = jnp.where(dx == 2, used, 0)
            a = a + is_first
            b = b + (used - is_first)
        return a, b

    a, b = lax.fori_loop(0, slots // 4, some, (jnp.int32(0), jnp.int32(second)))

    def fill(i, _):
        lists[a + i] = UNUSED
        lists[b + i] = UNUSED
        return 0

    lax.fori_loop(0, GROUP, fill, 0)
    lists[2 * second] = a
    lists[2 * second + 1] = b - second
    copy = pltpu.make_async_copy(lists, out.at[pl.ds(0, LISTS)], sem)
    copy.start()
    copy.wait()


def sort_tiles(*operands):
    smem = pl.BlockSpec(memory_space=pltpu.SMEM)
    return pl.pallas_call(
        sort_kernel,
        in_specs=[smem] * 4,
        out_specs=pl.BlockSpec(memory_space=pl.ANY),
        out_shape=jax.ShapeDtypeStruct((2**24,), jnp.int32),
        scratch_shapes=[pltpu.SMEM((LISTS,), jnp.int32), pltpu.SemaphoreType.DMA],
        cost_estimate=pl.CostEstimate(flops=0, bytes_accessed=2**12, transcendentals=0),
    )(*operands)


def join_kernel(token, *refs):
    for i, ref in enumerate(refs[:-1]):
        refs[-1][i * 16 : i * 16 + 16, :] = ref[...]


def join(token, *parts):
    spec = pl.BlockSpec(memory_space=pltpu.VMEM)
    return pl.pallas_call(
        join_kernel,
        in_specs=[pl.BlockSpec(memory_space=pl.ANY)] + [spec] * len(parts),
        out_specs=spec,
        out_shape=jax.ShapeDtypeStruct((16 * len(parts), parts[0].shape[1]), BF16),
        compiler_params=pltpu.CompilerParams(vmem_limit_bytes=4 * 2**20),
        cost_estimate=pl.CostEstimate(flops=0, bytes_accessed=2**18, transcendentals=0),
    )(token, *parts)


def tile_kernel(which, placed, lists, meta, source, mine, other, *rest):
    outs, (codes, tiles, wide, acc, list_sem, sems) = rest[: len(placed)], rest[len(placed) :]
    listed = pltpu.make_async_copy(lists.at[pl.ds(0, LISTS)], codes, list_sem)
    listed.start()
    for part, dist in enumerate((0,) + DISTS):
        y_of = (meta[0] - dist) & (YS - 1)
        for ref, core in ((mine, meta[1]), (other, 1 - meta[1])):
            at = pl.multiple_of((y_of * CS + core) * 16, 16)
            wide[pl.ds(at, 16), :] = ref[part * 16 : part * 16 + 16, :]
    for first, size in placed:

        def clear(i, _):
            acc[pl.ds(first + i * 4, 4)] = jnp.zeros((4, T, T), F32)
            return 0

        lax.fori_loop(0, size // 4, clear, 0)

    listed.wait()
    slots = source.shape[0]
    start = which * (slots + GROUP)
    groups = (codes[2 * (slots + GROUP) + which] + GROUP - 1) >> 5

    def bring(g, _):
        for u in range(GROUP):
            n = g * GROUP + u
            pltpu.make_async_copy(source.at[codes[start + n] >> 13], tiles.at[n], sems.at[g]).start()
        return 0

    lax.fori_loop(0, groups, bring, 0)
    def several(g, _):
        base = pl.multiple_of(g * GROUP, GROUP)
        here = tiles.at[pl.ds(base, GROUP)]
        pltpu.make_async_copy(source.at[pl.ds(0, GROUP)], here, sems.at[g]).wait()
        products = []
        for u in range(GROUP):
            at = pl.multiple_of(((codes[start + base + u] >> 8) & 31) * T, T)
            products.append(jnp.dot(wide[:, pl.ds(at, T)], tiles[base + u], preferred_element_type=F32))
        for u in range(GROUP):
            place = codes[start + base + u] & 255
            acc[place] = acc[place] + products[u]
        return 0

    lax.fori_loop(0, groups, several, 0)

    for out, (first, size) in zip(outs, placed):

        def put(i, _):
            out[pl.ds(i * 4, 4)] = acc[pl.ds(first + i * 4, 4)].astype(BF16)
            return 0

        lax.fori_loop(0, size // 4, put, 0)


def tile_products(which, placed, codes, meta, tiles, mine, other):
    smem, vmem = pl.BlockSpec(memory_space=pltpu.SMEM), pl.BlockSpec(memory_space=pltpu.VMEM)
    return pl.pallas_call(
        functools.partial(tile_kernel, which, placed),
        in_specs=[pl.BlockSpec(memory_space=pl.ANY), smem, pl.BlockSpec(memory_space=pl.ANY)] + [vmem] * 2,
        out_specs=[vmem] * len(placed),
        scratch_shapes=[
            pltpu.SMEM((LISTS,), jnp.int32),
            pltpu.VMEM(tiles.shape, BF16),
            pltpu.VMEM((T, mine.shape[1]), BF16),
            pltpu.VMEM((129, T, T), F32),
            pltpu.SemaphoreType.DMA,
            pltpu.SemaphoreType.DMA((tiles.shape[0] // GROUP,)),
        ],
        out_shape=[jax.ShapeDtypeStruct((n, T, T), BF16) for _, n in placed],
        compiler_params=pltpu.CompilerParams(vmem_limit_bytes=46 * 2**20),
        cost_estimate=pl.CostEstimate(flops=0, bytes_accessed=2**24, transcendentals=0),
    )(codes, meta, tiles, mine, other)


def middle_kernel(c0, upa, upb, downa, downb, feats, out, grad, sums, sems):
    copies = []
    for part in range(4):
        for k in range(part * 8, part * 8 + 8):
            up, down = (upa, downa) if k < 16 else (upb, downb)
            n = k % 16
            sums[k] = (c0[k].astype(F32) + up[n].astype(F32) + down[n].astype(F32)).astype(BF16)
        here = pl.ds(part * 8, 8)
        copies.append(pltpu.make_async_copy(sums.at[here], out.at[here], sems.at[part]))
        copies[-1].start()
    total = jnp.zeros((T, T), F32)
    for k in range(32):
        total += jnp.dot(sums[k], feats[k], preferred_element_type=F32)
    grad[...] = total.T
    for copy in copies:
        copy.wait()


def middle(*operands):
    spec = pl.BlockSpec(memory_space=pltpu.VMEM)
    return pl.pallas_call(
        middle_kernel,
        in_specs=[spec] * 6,
        out_specs=[pl.BlockSpec(memory_space=pl.ANY), spec],
        out_shape=[jax.ShapeDtypeStruct((32, T, T), BF16), jax.ShapeDtypeStruct((T, T), F32)],
        scratch_shapes=[pltpu.VMEM((32, T, T), BF16), pltpu.SemaphoreType.DMA((4,))],
        compiler_params=pltpu.CompilerParams(vmem_limit_bytes=12 * 2**20),
        cost_estimate=pl.CostEstimate(flops=2**27, bytes_accessed=5 * 2**20, transcendentals=0),
    )(*operands)


def last_kernel(aggregate, weight, grad, more, importance, delta, input_grad, importance_out):
    importance_out[...] = importance[...] - (grad[...] + more[...]) * delta[...]
    for q in range(4):
        product = jnp.dot(weight[...], aggregate[q], preferred_element_type=F32)
        input_grad[q * T : q * T + T, :] = product.T.astype(BF16)


def last(*operands):
    spec = pl.BlockSpec(memory_space=pltpu.VMEM)
    return pl.pallas_call(
        last_kernel,
        in_specs=[spec] * 6,
        out_specs=[spec] * 2,
        out_shape=[jax.ShapeDtypeStruct((4 * T, T), BF16), jax.ShapeDtypeStruct((T, T), F32)],
        compiler_params=pltpu.CompilerParams(vmem_limit_bytes=4 * 2**20),
        cost_estimate=pl.CostEstimate(flops=2**24, bytes_accessed=2**19, transcendentals=0),
    )(*operands)


def add(*values):
    return sum(v.astype(F32) for v in values).astype(BF16)


def local(tile_vals, tile_row, tile_col, tile_count, out_grad, relu_mask, features, weight, importance, weight_delta):
    x, y, core = (lax.axis_index(a) for a in ("x", "y", "core"))
    slots = tile_vals.shape[2]
    wide_feats = lax.all_gather(features, "z", axis=0, tiled=True).reshape(ZS * 4, T, T)

    masked = (out_grad.astype(F32) * relu_mask.astype(F32)).astype(BF16).T
    codes = sort_tiles(tile_row.reshape(slots), tile_col.reshape(slots), tile_count.reshape(1), x.reshape(1))
    meta = jnp.stack([y, core]).astype(jnp.int32)

    mine = join(codes, masked, *(shift(masked, "y", YS, d) for d in DISTS))
    operands = (codes, meta, tile_vals.reshape(slots, T, T), mine, swap(mine))
    c2a, c2b = tile_products(0, CHUNK2, *operands)
    c1b, c3a, c1a, c3b, c0 = tile_products(1, OTHERS, *operands)

    up, down = shift(c2a, "x", XS, 1), shift(c2b, "x", XS, 3)
    upb, downa = shift(c1b, "x", XS, 1), shift(c3a, "x", XS, 3)
    upa, downb = shift(add(c1a, up), "x", XS, 1), shift(add(c3b, down), "x", XS, 3)
    reduced, grad = middle(fetch(c0), upa, upb, downa, downb, fetch(wide_feats))

    aggregate = lax.psum_scatter(reduced, "z", scatter_dimension=0, tiled=True)

    grad = grad + swap(grad)
    grad = grad + shift(grad, "y", YS, 2) + shift(grad, "y", YS, 1) + shift(grad, "y", YS, 3)
    grad = grad + shift(grad, "x", XS, 2) + shift(grad, "x", XS, 1) + shift(grad, "x", XS, 3)
    grad = spread(grad, "z", ZS, ((1, 7), (2, 6), (3, 5), (4, None)), core)
    return last(aggregate, weight, grad, swap(grad), importance, weight_delta)


def solution(mesh):
    mesh = Mesh(mesh.devices.reshape(XS, ZS, YS, CS), ("x", "z", "y", "core"))
    row, col = ("x", "z"), ("y", "core")
    return jax.shard_map(
        local,
        mesh=mesh,
        in_specs=(
            P(row, col, None, None, None),
            P(row, col, None),
            P(row, col, None),
            P(row, col),
            P(row, col),
            P(row, col),
            P(row + col, None),
            P(),
            P(),
            P(),
        ),
        out_specs=(P(row + col, None), P()),
        check_vma=False,
    )
```
